32 devices in a mesh: dp: 4 (over x, core), fsdp: 4 (over z), sp: 2 (over y).
Axes of the slice: x: 2, y: 2, z: 4, core: 2. Of those that a mesh axis runs over, the one named last changes fastest.
Arguments:
- query_raw: bfloat16 [4, 1024, 5120], P('dp', ('fsdp', 'sp')), may hold values from -35 to 35
- query_tangent: bfloat16 [4, 1024, 5120], P('dp', ('fsdp', 'sp')), may hold values from -35 to 35
- key_raw: bfloat16 [4, 512, 5120], P('dp', 'fsdp', 'sp'), may hold values from -40 to 40
- value_text: bfloat16 [4, 512, 5120], P('dp', 'fsdp', 'sp'), may hold values from -6 to 6
- query_gain: float32 [5120], replicated, may hold values from 0.25 to 1.75
- key_gain: float32 [5120], P('sp'), may hold values from 0.25 to 1.75
Outputs:
- attn_tangent: bfloat16 [4, 1024, 5120], P('dp', ('fsdp', 'sp'))
The draws below stay inside these ranges and needn't reach their ends.
All inputs are finite; a program needn't handle non-finite values.
Results may differ from the reference program's by a relative error of at most 0.012.
The reference program's roundings to bfloat16 on the way count: a program that leaves them out, or rounds other values in their place, can miss the bound.
Values may be sent and summed in bfloat16 or wider, within the bound.
A program may use at most 64 MiB of HBM per device.

```python
import jax
import jax.numpy as jnp
from jax import lax

D = 5120
H = 40
HD = 128
CTX = 512
SEQ = 1024
CLIPS = 4


def scaled_field(key, leading, row_count, column_count, column_spread, ramp):
    subkeys = jax.random.split(key, 4)
    normal_part = jnp.clip(jax.random.normal(subkeys[0], (leading, row_count, column_count), jnp.float32), -3.0, 3.0)
    centered = normal_part
    row_scale = jnp.exp(jax.random.uniform(subkeys[2], (leading, row_count, 1), jnp.float32, -1.15, 1.15))
    position = jnp.arange(column_count, dtype=jnp.float32) / column_count - 0.5
    column_log = jax.random.uniform(subkeys[3], (leading, 1, column_count), jnp.float32, -column_spread, column_spread)
    column_scale = jnp.exp(column_log + ramp * position)
    return centered * row_scale * column_scale


def draw_query_raw(key, part):
    key = jax.random.fold_in(key, 11)
    drawn = scaled_field(key, CLIPS, SEQ, D, 1.15, 0.0)
    return drawn.astype(jnp.bfloat16)


def draw_key_raw(key, part):
    key = jax.random.fold_in(key, 12)
    drawn = scaled_field(key, CLIPS, CTX, D, 0.6, 1.1)
    return drawn.astype(jnp.bfloat16)


def draw_query_tangent(key, part):
    key = jax.random.fold_in(key, 13)
    drawn = scaled_field(key, CLIPS, SEQ, D, 1.15, 0.0)
    return drawn.astype(jnp.bfloat16)


def levels(rng, extent, shards, smallest, largest):
    level = 1.0
    for dim, blocks in shards:
        heights = jax.random.uniform(jax.random.fold_in(jax.random.fold_in(rng, 6), dim), (blocks,), jnp.float32, smallest / len(shards), largest / len(shards))
        level = level * jnp.repeat(jnp.exp(heights), extent[dim] // blocks).reshape((-1,) + (1,) * (len(extent) - 1 - dim))
    return level


def gaussian(rng, extent, deviation, bound, cuts=(), held_as=jnp.bfloat16):
    values = jax.random.normal(rng, extent, jnp.float32) * deviation
    if len(cuts) > 0:
        values = levels(rng, extent, cuts, -0.22, 0.18) * values
    return jnp.clip(values, min=-bound, max=bound).astype(held_as)


def setup_inputs(seed: int = 0) -> dict:
    key_of = jax.random.split(jax.random.key(seed), 7)
    query_raw = draw_query_raw(jax.random.fold_in(key_of[6], 71), 0)
    query_tangent = draw_query_tangent(jax.random.fold_in(key_of[6], 71), 0)
    key_raw = draw_key_raw(jax.random.fold_in(key_of[6], 71), 0)
    value_text = gaussian(key_of[3], (CLIPS, CTX, D), 1.0, 6.0, ((0, 4), (1, 4), (2, 2)))
    query_gain = jnp.clip(1.0 + 0.15 * jax.random.normal(key_of[4], (D,), jnp.float32), 0.25, 1.75)
    key_gain = jnp.clip(1.0 + 0.15 * jax.random.normal(key_of[5], (D,), jnp.float32), 0.25, 1.75)
    return dict(query_raw=query_raw, query_tangent=query_tangent, key_raw=key_raw, value_text=value_text, query_gain=query_gain, key_gain=key_gain)


epsilon = 1e-06

def norm_tangent(source, tangent, gain):
    floats = source.astype(jnp.float32)
    moving = tangent.astype(jnp.float32)
    inverse = lax.rsqrt(lax.optimization_barrier(jnp.mean(floats * floats, axis=-1, keepdims=True)) + epsilon)
    projected = lax.optimization_barrier(jnp.mean(floats * moving, axis=-1, keepdims=True))
    primal_rows = (floats * inverse * gain).astype(jnp.bfloat16)
    tangent_rows = (gain * inverse * (moving - floats * inverse * inverse * projected)).astype(jnp.bfloat16)
    return (primal_rows, tangent_rows)

def norm_rows(source, gain):
    floats = source.astype(jnp.float32)
    inverse = lax.rsqrt(lax.optimization_barrier(jnp.mean(floats * floats, axis=-1, keepdims=True)) + epsilon)
    return (floats * inverse * gain).astype(jnp.bfloat16)

def head_tangent(entries):
    query_head, tangent_head, key_head, value_head = entries
    scale = HD ** (-0.5)
    scores = jnp.dot(query_head, key_head.T, preferred_element_type=jnp.float32) * scale
    slopes = jnp.dot(tangent_head, key_head.T, preferred_element_type=jnp.float32) * scale
    probs = jax.nn.softmax(scores, axis=-1)
    slope_mean = lax.optimization_barrier(jnp.sum(probs * slopes, axis=-1, keepdims=True))
    value_float = value_head.astype(jnp.float32)
    primal_out = jnp.dot(probs, value_float, precision=lax.Precision.HIGHEST)
    bent = jnp.dot(probs * slopes, value_float, precision=lax.Precision.HIGHEST)
    return bent - slope_mean * primal_out

def clip_tangent(operands):
    query_raw, query_tangent, key_rows, value_rows, query_gain = operands
    query_rows, tangent_rows = norm_tangent(query_raw, query_tangent, query_gain)
    query_heads = query_rows.reshape(SEQ, H, HD).transpose(1, 0, 2)
    tangent_heads = tangent_rows.reshape(SEQ, H, HD).transpose(1, 0, 2)
    key_heads = key_rows.reshape(CTX, H, HD).transpose(1, 0, 2)
    value_heads = value_rows.reshape(CTX, H, HD).transpose(1, 0, 2)
    heads_out = lax.map(head_tangent, (query_heads, tangent_heads, key_heads, value_heads))
    return heads_out.transpose(1, 0, 2).reshape(SEQ, D).astype(jnp.bfloat16)

def reference(query_raw, query_tangent, key_raw, value_text, query_gain, key_gain):
    key_rows = norm_rows(key_raw, key_gain)
    gains = jnp.broadcast_to(query_gain, (CLIPS, D))
    return lax.map(clip_tangent, (query_raw, query_tangent, key_rows, value_text, gains))
```

```python
import functools

import jax
import jax.numpy as jnp
from jax import lax
from jax.experimental import pallas as pl
from jax.experimental.pallas import tpu as pltpu
from jax.sharding import PartitionSpec as P

HD = 128
epsilon = 1e-06
MESH = pl.DeviceIdType.MESH


def choose_groups(heads):
    for count in (5, 4, 3, 2):
        if heads % count == 0:
            return count
    return 1


def kernel(
    n, s, groups,
    qr_ref, qt_ref, kr_ref, v_ref, qg_ref, kg_ref, out_ref,
    kbuf, vbuf, qsend, qbuf, obuf, ssbuf,
    vload_sem, kv_send, kv_recv, q_send, q_recv, ss_send, ss_recv, o_send, o_recv, own_sem,
):
    t, d = qr_ref.shape
    c, fl = kr_ref.shape
    fg = fl // groups
    per_group = fg // HD
    r = lax.axis_index("fsdp")
    p = lax.axis_index("sp")
    bufs = (kbuf, vbuf)

    def peer(dj):
        return lax.rem(p + dj, s)

    def origin(dj):
        return lax.rem(p + s - dj, s)

    def vload(g):
        columns = pl.ds(g * fg, fg)
        return pltpu.make_async_copy(v_ref.at[:, columns], vbuf.at[g, r], vload_sem.at[g])

    def piece(kind, g, src, way):
        target = r - 1 if way == 0 else r + 1
        buf = bufs[kind]
        return pltpu.make_async_remote_copy(
            src_ref=buf.at[g, src],
            dst_ref=buf.at[g, src],
            send_sem=kv_send.at[kind, way, g, src],
            recv_sem=kv_recv.at[kind, g, src],
            device_id={"fsdp": target},
            device_id_type=MESH,
        )

    def sums(dj):
        return pltpu.make_async_remote_copy(
            src_ref=ssbuf.at[0],
            dst_ref=ssbuf.at[dj],
            send_sem=ss_send.at[dj - 1],
            recv_sem=ss_recv.at[dj - 1],
            device_id={"sp": peer(dj)},
            device_id_type=MESH,
        )

    def queries(g, dj):
        return pltpu.make_async_remote_copy(
            src_ref=qsend.at[dj - 1, g],
            dst_ref=qbuf.at[g, dj],
            send_sem=q_send.at[g, dj - 1],
            recv_sem=q_recv.at[g, dj - 1],
            device_id={"sp": peer(dj)},
            device_id_type=MESH,
        )

    def output(g, dj):
        columns = pl.ds(pl.multiple_of(p * fl + g * fg, HD), fg)
        return pltpu.make_async_remote_copy(
            src_ref=obuf.at[g, dj],
            dst_ref=out_ref.at[:, columns],
            send_sem=o_send.at[g, dj - 1],
            recv_sem=o_recv.at[g, dj - 1],
            device_id={"sp": origin(dj)},
            device_id_type=MESH,
        )

    def own_output(g):
        columns = pl.ds(pl.multiple_of(p * fl + g * fg, HD), fg)
        return pltpu.make_async_copy(obuf.at[g, 0], out_ref.at[:, columns], own_sem.at[g])

    has_left = r > 0
    has_right = r < n - 1

    barrier = pltpu.get_barrier_semaphore()
    for dj in range(1, s):
        pl.semaphore_signal(barrier, inc=1, device_id={"sp": peer(dj)}, device_id_type=MESH)

    @pl.when(has_left)
    def _():
        pl.semaphore_signal(barrier, inc=1, device_id={"fsdp": r - 1}, device_id_type=MESH)

    @pl.when(has_right)
    def _():
        pl.semaphore_signal(barrier, inc=1, device_id={"fsdp": r + 1}, device_id_type=MESH)

    for g in range(groups):
        vload(g).start()

    acc = jnp.zeros((c, HD), jnp.float32)
    for i in range(fl // HD):
        x = kr_ref[:, i * HD:(i + 1) * HD].astype(jnp.float32)
        acc = acc + x * x
    ssbuf[0] = jnp.broadcast_to(jnp.sum(acc, axis=-1, keepdims=True), (c, HD))

    pl.semaphore_wait(barrier, s - 1 + has_left.astype(jnp.int32) + has_right.astype(jnp.int32))

    for dj in range(1, s):
        sums(dj).start()
    for g in range(groups):
        vload(g).wait()

    def send_own(kind, g):
        @pl.when(has_left)
        def _():
            piece(kind, g, r, 0).start()

        @pl.when(has_right)
        def _():
            piece(kind, g, r, 1).start()

    ahead = min(2, groups)
    for g in range(ahead):
        send_own(1, g)

    for dj in range(1, s):
        sums(dj).wait_recv()
    total = ssbuf[0]
    for dj in range(1, s):
        total = total + ssbuf[dj]
    key_inverse = lax.rsqrt(total * (1.0 / d) + epsilon)
    for g in range(groups):
        for i in range(per_group):
            lo = g * fg + i * HD
            x = kr_ref[:, lo:lo + HD].astype(jnp.float32)
            kbuf[g, r, :, i * HD:(i + 1) * HD] = (
                x * key_inverse * kg_ref[:, lo:lo + HD]
            ).astype(jnp.bfloat16)
        if g < ahead:
            send_own(0, g)

    square = jnp.zeros((t, HD), jnp.float32)
    cross = jnp.zeros((t, HD), jnp.float32)
    for i in range(d // HD):
        x = qr_ref[:, i * HD:(i + 1) * HD].astype(jnp.float32)
        y = qt_ref[:, i * HD:(i + 1) * HD].astype(jnp.float32)
        square = square + x * x
        cross = cross + x * y
    inverse = lax.rsqrt(jnp.sum(square, axis=-1, keepdims=True) * (1.0 / d) + epsilon)
    along = jnp.sum(cross, axis=-1, keepdims=True) * (1.0 / d)
    bend = inverse * inverse * along
    inverse = jnp.broadcast_to(inverse, (t, HD))
    bend = jnp.broadcast_to(bend, (t, HD))

    def norm_group(g, carry):
        for dj in [*range(1, s), 0]:
            j = peer(dj)
            for i in range(per_group):
                columns = pl.ds(pl.multiple_of(j * fl + g * fg + i * HD, HD), HD)
                x = qr_ref[:, columns].astype(jnp.float32)
                y = qt_ref[:, columns].astype(jnp.float32)
                gain = qg_ref[:, columns]
                primal = (x * inverse * gain).astype(jnp.bfloat16)
                tangent = (gain * inverse * (y - x * bend)).astype(jnp.bfloat16)
                if dj == 0:
                    qbuf[g, 0, 0, :, i * HD:(i + 1) * HD] = primal
                    qbuf[g, 0, 1, :, i * HD:(i + 1) * HD] = tangent
                else:
                    qsend[dj - 1, g, 0, :, i * HD:(i + 1) * HD] = primal
                    qsend[dj - 1, g, 1, :, i * HD:(i + 1) * HD] = tangent
            if dj > 0:
                queries(g, dj).start()
        return carry

    lax.fori_loop(0, groups, norm_group, 0)

    scale = HD ** (-0.5)

    def attend(g):
        for i in range(per_group):
            columns = slice(i * HD, (i + 1) * HD)
            keys = kbuf[g, :, :, columns].reshape(n * c, HD)
            values = vbuf[g, :, :, columns].reshape(n * c, HD)
            for dj in range(s):
                rows = qbuf[g, dj, :, :, columns].reshape(2 * t, HD)
                paired = lax.dot_general(
                    rows, keys, (((1,), (1,)), ((), ())), preferred_element_type=jnp.float32
                )
                scores, slopes = paired[:t], paired[t:]
                top = jnp.max(scores, axis=-1, keepdims=True)
                weights = jnp.exp((scores - top) * scale)
                whole = jnp.sum(weights, axis=-1, keepdims=True)
                mean = jnp.sum(weights * slopes, axis=-1, keepdims=True) / whole
                tilted = weights * (slopes - mean)
                high = tilted.astype(jnp.bfloat16)
                low = (tilted - high.astype(jnp.float32)).astype(jnp.bfloat16)
                result = jnp.dot(high, values, preferred_element_type=jnp.float32)
                result = result + jnp.dot(low, values, preferred_element_type=jnp.float32)
                obuf[g, dj, :, columns] = (result * (scale / whole)).astype(jnp.bfloat16)

    def step(g, carry):
        @pl.when(g + ahead < groups)
        def _():
            send_own(1, g + ahead)
            send_own(0, g + ahead)

        for h in range(1, n):
            for kind in (1, 0):
                @pl.when(r + h < n)
                def _():
                    piece(kind, g, r + h, 0).wait_recv()

                    @pl.when(has_left)
                    def _():
                        piece(kind, g, r + h, 0).start()

                @pl.when(r - h >= 0)
                def _():
                    piece(kind, g, r - h, 1).wait_recv()

                    @pl.when(has_right)
                    def _():
                        piece(kind, g, r - h, 1).start()

        for dj in range(1, s):
            queries(g, dj).wait_recv()
        attend(g)
        own_output(g).start()
        for dj in range(1, s):
            output(g, dj).start()
        return carry

    lax.fori_loop(0, groups, step, 0)

    for dj in range(1, s):
        sums(dj).wait_send()

    def finish(g, carry):
        for kind in (1, 0):
            for h in range(n):
                @pl.when(jnp.logical_and(r + h < n, has_left))
                def _():
                    piece(kind, g, r + h, 0).wait_send()

                @pl.when(jnp.logical_and(r - h >= 0, has_right))
                def _():
                    piece(kind, g, r - h, 1).wait_send()
        own_output(g).wait()
        for dj in range(1, s):
            queries(g, dj).wait_send()
            output(g, dj).wait_send()
            output(g, dj).wait_recv()
        return carry

    lax.fori_loop(0, groups, finish, 0)


def shards(n, s, query_raw, query_tangent, key_raw, value_text, query_gain, key_gain):
    _, t, d = query_raw.shape
    _, c, fl = key_raw.shape
    groups = choose_groups(fl // HD)
    fg = fl // groups
    peers = max(s - 1, 1)
    vmem = pl.BlockSpec(memory_space=pltpu.VMEM)
    anywhere = pl.BlockSpec(memory_space=pl.ANY)
    flops = 2 * 4 * s * t * n * c * fl
    moved = 2 * (3 * t * d + 2 * c * fl)
    result = pl.pallas_call(
        functools.partial(kernel, n, s, groups),
        out_shape=jax.ShapeDtypeStruct((t, d), jnp.bfloat16),
        in_specs=[vmem, vmem, vmem, anywhere, vmem, vmem],
        out_specs=anywhere,
        scratch_shapes=[
            pltpu.VMEM((groups, n, c, fg), jnp.bfloat16),
            pltpu.VMEM((groups, n, c, fg), jnp.bfloat16),
            pltpu.VMEM((peers, groups, 2, t, fg), jnp.bfloat16),
            pltpu.VMEM((groups, s, 2, t, fg), jnp.bfloat16),
            pltpu.VMEM((groups, s, t, fg), jnp.bfloat16),
            pltpu.VMEM((s, c, HD), jnp.float32),
            pltpu.SemaphoreType.DMA((groups,)),
            pltpu.SemaphoreType.DMA((2, 2, groups, n)),
            pltpu.SemaphoreType.DMA((2, groups, n)),
            pltpu.SemaphoreType.DMA((groups, peers)),
            pltpu.SemaphoreType.DMA((groups, peers)),
            pltpu.SemaphoreType.DMA((peers,)),
            pltpu.SemaphoreType.DMA((peers,)),
            pltpu.SemaphoreType.DMA((groups, peers)),
            pltpu.SemaphoreType.DMA((groups, peers)),
            pltpu.SemaphoreType.DMA((groups,)),
        ],
        compiler_params=pltpu.CompilerParams(
            collective_id=0, has_side_effects=True, vmem_limit_bytes=44 * 1024 * 1024
        ),
        cost_estimate=pl.CostEstimate(
            flops=flops, bytes_accessed=moved, transcendentals=s * t * n * c * (fl // HD)
        ),
    )(
        query_raw[0], query_tangent[0], key_raw[0], value_text[0],
        query_gain[None], key_gain[None],
    )
    return result[None]


def solution(mesh):
    n, s = mesh.shape["fsdp"], mesh.shape["sp"]
    return jax.shard_map(
        functools.partial(shards, n, s),
        mesh=mesh,
        in_specs=(
            P("dp", ("fsdp", "sp"), None),
            P("dp", ("fsdp", "sp"), None),
            P("dp", "fsdp", "sp"),
            P("dp", "fsdp", "sp"),
            P(),
            P("sp"),
        ),
        out_specs=P("dp", ("fsdp", "sp"), None),
        check_vma=False,
    )
```

```python
import functools

import jax
import jax.numpy as jnp
from jax import lax
from jax.experimental import pallas as pl
from jax.experimental.pallas import tpu as pltpu
from jax.sharding import PartitionSpec as P

HD = 128
epsilon = 1e-06
MESH = pl.DeviceIdType.MESH


def choose_groups(heads):
    for count in (10, 8, 6, 5, 4, 3, 2):
        if heads % count == 0:
            return count
    return 1


def kernel(
    n, s, groups,
    qr_hbm, qt_hbm, kr_hbm, v_ref, qg_hbm, kg_hbm, out_ref,
    qr_ref, qt_ref, kr_ref, qg_ref, kg_ref,
    kbuf, vbuf, qsend, qbuf, xbuf, obuf, ybuf, ssbuf,
    load_sem, vload_sem, kv_send, kv_recv, q_send, q_recv, x_send, x_recv,
    ss_send, ss_recv, o_send, o_recv, y_send, own_sem,
):
    t, d = qr_ref.shape
    inputs = ((kr_hbm, kr_ref), (kg_hbm, kg_ref), (qr_hbm, qr_ref), (qt_hbm, qt_ref), (qg_hbm, qg_ref))
    c, fl = kr_ref.shape
    fg = fl // groups
    per_group = fg // HD
    r = lax.axis_index("fsdp")
    p = lax.axis_index("sp")
    bufs = (kbuf, vbuf)
    partner = jnp.where(r == 0, 1, jnp.where(r == 1, 0, jnp.where(r == n - 1, n - 2, n - 1)))

    def peer(dj):
        return lax.rem(p + dj, s)

    def origin(dj):
        return lax.rem(p + s - dj, s)

    def vload(g):
        columns = pl.ds(g * fg, fg)
        return pltpu.make_async_copy(v_ref.at[:, columns], vbuf.at[g, r], vload_sem.at[g])

    def piece(kind, g, src, way):
        target = r - 1 if way == 0 else r + 1
        buf = bufs[kind]
        return pltpu.make_async_remote_copy(
            src_ref=buf.at[g, src],
            dst_ref=buf.at[g, src],
            send_sem=kv_send.at[kind, way, g, src],
            recv_sem=kv_recv.at[kind, g, src],
            device_id={"fsdp": target},
            device_id_type=MESH,
        )

    def sums(dj):
        return pltpu.make_async_remote_copy(
            src_ref=ssbuf.at[0],
            dst_ref=ssbuf.at[dj],
            send_sem=ss_send.at[dj - 1],
            recv_sem=ss_recv.at[dj - 1],
            device_id={"sp": peer(dj)},
            device_id_type=MESH,
        )

    def queries(g, dj):
        return pltpu.make_async_remote_copy(
            src_ref=qsend.at[dj - 1, g],
            dst_ref=qbuf.at[g, dj],
            send_sem=q_send.at[g, dj - 1],
            recv_sem=q_recv.at[g, dj - 1],
            device_id={"sp": peer(dj)},
            device_id_type=MESH,
        )

    def lend(g, dj):
        return pltpu.make_async_remote_copy(
            src_ref=qbuf.at[g, dj],
            dst_ref=xbuf.at[g // 2, dj],
            send_sem=x_send.at[g // 2, dj],
            recv_sem=x_recv.at[g // 2, dj],
            device_id={"fsdp": partner},
            device_id_type=MESH,
        )

    def give_back(g, dj):
        columns = pl.ds(pl.multiple_of(p * fl + g * fg, HD), fg)
        return pltpu.make_async_remote_copy(
            src_ref=ybuf.at[g // 2, dj],
            dst_ref=out_ref.at[:, columns],
            send_sem=y_send.at[g // 2, dj],
            recv_sem=o_recv.at[g, dj],
            device_id={"fsdp": partner, "sp": origin(dj)},
            device_id_type=MESH,
        )

    def output(g, dj):
        columns = pl.ds(pl.multiple_of(p * fl + g * fg, HD), fg)
        return pltpu.make_async_remote_copy(
            src_ref=obuf.at[g, dj],
            dst_ref=out_ref.at[:, columns],
            send_sem=o_send.at[g, dj - 1],
            recv_sem=o_recv.at[g, dj],
            device_id={"sp": origin(dj)},
            device_id_type=MESH,
        )

    def own_output(g):
        columns = pl.ds(pl.multiple_of(p * fl + g * fg, HD), fg)
        return pltpu.make_async_copy(obuf.at[g, 0], out_ref.at[:, columns], own_sem.at[g])

    has_left = r > 0
    has_right = r < n - 1
    lending = n >= 4
    is_end = jnp.logical_or(r == 0, r == n - 1) if lending else r < 0
    is_helper = jnp.logical_or(r == 1, r == n - 2) if lending else r < 0

    def lent(g):
        return lax.rem(jnp.int32(g), 2) == 0

    def goes_left(g):
        return r > jnp.where(lent(g), 1, 0) if lending else has_left

    def goes_right(g):
        return r < jnp.where(lent(g), n - 2, n - 1) if lending else has_right

    def receives(g):
        return jnp.logical_not(jnp.logical_and(is_end, lent(g)))

    barrier = pltpu.get_barrier_semaphore()
    for dj in range(1, s):
        pl.semaphore_signal(barrier, inc=1, device_id={"sp": peer(dj)}, device_id_type=MESH)

    @pl.when(has_left)
    def _():
        pl.semaphore_signal(barrier, inc=1, device_id={"fsdp": r - 1}, device_id_type=MESH)

    @pl.when(has_right)
    def _():
        pl.semaphore_signal(barrier, inc=1, device_id={"fsdp": r + 1}, device_id_type=MESH)

    if s > 1:
        @pl.when(is_end)
        def _():
            for dj in range(1, s):
                pl.semaphore_signal(
                    barrier, inc=1, device_id={"fsdp": partner, "sp": peer(dj)}, device_id_type=MESH
                )

    loads = [pltpu.make_async_copy(a, b, load_sem.at[i]) for i, (a, b) in enumerate(inputs)]
    loads[0].start()
    for g in range(groups):
        vload(g).start()
    for load in loads[1:]:
        load.start()
    loads[0].wait()

    acc = jnp.zeros((c, HD), jnp.float32)
    for i in range(fl // HD):
        x = kr_ref[:, i * HD:(i + 1) * HD].astype(jnp.float32)
        acc = acc + x * x
    ssbuf[0] = jnp.broadcast_to(jnp.sum(acc, axis=-1, keepdims=True), (c, HD))

    pl.semaphore_wait(
        barrier,
        s - 1
        + has_left.astype(jnp.int32)
        + has_right.astype(jnp.int32)
        + (s - 1) * is_helper.astype(jnp.int32),
    )

    for dj in range(1, s):
        sums(dj).start()
    for g in range(groups):
        vload(g).wait()

    def send_own(kind, g):
        @pl.when(goes_left(g))
        def _():
            piece(kind, g, r, 0).start()

        @pl.when(goes_right(g))
        def _():
            piece(kind, g, r, 1).start()

    ahead = min(4, groups)
    for g in range(ahead):
        send_own(1, g)

    for dj in range(1, s):
        sums(dj).wait_recv()
    total = ssbuf[0]
    for dj in range(1, s):
        total = total + ssbuf[dj]
    loads[1].wait()
    key_inverse = lax.rsqrt(total * (1.0 / d) + epsilon)
    for g in range(groups):
        for i in range(per_group):
            lo = g * fg + i * HD
            x = kr_ref[:, lo:lo + HD].astype(jnp.float32)
            kbuf[g, r, :, i * HD:(i + 1) * HD] = (
                x * key_inverse * kg_ref[lo:lo + HD].reshape(1, HD)
            ).astype(jnp.bfloat16)
        if g < ahead:
            send_own(0, g)

    for load in loads[2:]:
        load.wait()
    square = jnp.zeros((t, HD), jnp.float32)
    cross = jnp.zeros((t, HD), jnp.float32)
    for i in range(d // HD):
        x = qr_ref[:, i * HD:(i + 1) * HD].astype(jnp.float32)
        y = qt_ref[:, i * HD:(i + 1) * HD].astype(jnp.float32)
        square = square + x * x
        cross = cross + x * y
    inverse = lax.rsqrt(jnp.sum(square, axis=-1, keepdims=True) * (1.0 / d) + epsilon)
    along = jnp.sum(cross, axis=-1, keepdims=True) * (1.0 / d)
    bend = inverse * inverse * along
    inverse = jnp.broadcast_to(inverse, (t, HD))
    bend = jnp.broadcast_to(bend, (t, HD))

    def norm_group(g, carry):
        for dj in [*range(1, s), 0]:
            j = peer(dj)
            for i in range(per_group):
                columns = pl.ds(pl.multiple_of(j * fl + g * fg + i * HD, HD), HD)
                x = qr_ref[:, columns].astype(jnp.float32)
                y = qt_ref[:, columns].astype(jnp.float32)
                gain = qg_ref[:, columns]
                primal = (x * inverse * gain).astype(jnp.bfloat16)
                tangent = (gain * inverse * (y - x * bend)).astype(jnp.bfloat16)
                if dj == 0:
                    qbuf[g, 0, 0, :, i * HD:(i + 1) * HD] = primal
                    qbuf[g, 0, 1, :, i * HD:(i + 1) * HD] = tangent
                else:
                    qsend[dj - 1, g, 0, :, i * HD:(i + 1) * HD] = primal
                    qsend[dj - 1, g, 1, :, i * HD:(i + 1) * HD] = tangent
            if dj > 0:
                queries(g, dj).start()
        return carry

    lax.fori_loop(0, groups, norm_group, 0)

    scale = HD ** (-0.5)

    def attend(g, rows_ref, place, into_ref, where):
        for i in range(per_group):
            columns = slice(i * HD, (i + 1) * HD)
            keys = kbuf[g, :, :, columns].reshape(n * c, HD)
            values = vbuf[g, :, :, columns].reshape(n * c, HD)
            for dj in range(s):
                rows = rows_ref[place, dj, :, :, columns].reshape(2 * t, HD)
                paired = lax.dot_general(
                    rows, keys, (((1,), (1,)), ((), ())), preferred_element_type=jnp.float32
                )
                scores, slopes = paired[:t], paired[t:]
                top = jnp.max(scores, axis=-1, keepdims=True)
                weights = jnp.exp((scores - top) * scale)
                whole = jnp.sum(weights, axis=-1, keepdims=True)
                mean = jnp.sum(weights * slopes, axis=-1, keepdims=True) / whole
                tilted = weights * (slopes - mean)
                high = tilted.astype(jnp.bfloat16)
                low = (tilted - high.astype(jnp.float32)).astype(jnp.bfloat16)
                result = jnp.dot(high, values, preferred_element_type=jnp.float32)
                result = result + jnp.dot(low, values, preferred_element_type=jnp.float32)
                into_ref[where, dj, :, columns] = (result * (scale / whole)).astype(jnp.bfloat16)

    def launch(g):
        send_own(1, g)
        send_own(0, g)

    def lend_group(g):
        @pl.when(jnp.logical_and(is_end, lent(g)))
        def _():
            for dj in range(s):
                if dj > 0:
                    queries(g, dj).wait_recv()
                lend(g, dj).start()

    def forward(g):
        for h in range(1, n):
            for kind in (1, 0):
                @pl.when(jnp.logical_and(r + h < n, receives(g)))
                def _():
                    piece(kind, g, r + h, 0).wait_recv()

                    @pl.when(goes_left(g))
                    def _():
                        piece(kind, g, r + h, 0).start()

                @pl.when(jnp.logical_and(r - h >= 0, receives(g)))
                def _():
                    piece(kind, g, r - h, 1).wait_recv()

                    @pl.when(goes_right(g))
                    def _():
                        piece(kind, g, r - h, 1).start()

    def work(g):
        @pl.when(receives(g))
        def _():
            for dj in range(1, s):
                queries(g, dj).wait_recv()
            attend(g, qbuf, g, obuf, g)
            own_output(g).start()
            for dj in range(1, s):
                output(g, dj).start()

        @pl.when(jnp.logical_and(is_helper, lent(g)))
        def _():
            for dj in range(s):
                lend(g, dj).wait_recv()
            attend(g, xbuf, g // 2, ybuf, g // 2)
            for dj in range(s):
                give_back(g, dj).start()

    for g in range(ahead):
        lend_group(g)

    lead = 1

    def step(i, carry):
        @pl.when(i + ahead < groups)
        def _():
            launch(i + ahead)
            lend_group(i + ahead)

        @pl.when(i < groups)
        def _():
            forward(i)

        @pl.when(i >= lead)
        def _():
            work(i - lead)

        return carry

    lax.fori_loop(0, groups + lead, step, 0)

    for dj in range(1, s):
        sums(dj).wait_send()

    def finish(g, carry):
        for kind in (1, 0):
            for h in range(n):
                @pl.when(jnp.logical_and(r + h < n, goes_left(g)) if h == 0 else
                         jnp.logical_and(jnp.logical_and(r + h < n, goes_left(g)), receives(g)))
                def _():
                    piece(kind, g, r + h, 0).wait_send()

                @pl.when(jnp.logical_and(r - h >= 0, goes_right(g)) if h == 0 else
                         jnp.logical_and(jnp.logical_and(r - h >= 0, goes_right(g)), receives(g)))
                def _():
                    piece(kind, g, r - h, 1).wait_send()

        for dj in range(1, s):
            queries(g, dj).wait_send()
            output(g, dj).wait_recv()

        @pl.when(receives(g))
        def _():
            own_output(g).wait()
            for dj in range(1, s):
                output(g, dj).wait_send()

        @pl.when(jnp.logical_and(is_end, lent(g)))
        def _():
            for dj in range(s):
                lend(g, dj).wait_send()
            give_back(g, 0).wait_recv()

        @pl.when(jnp.logical_and(is_helper, lent(g)))
        def _():
            for dj in range(s):
                give_back(g, dj).wait_send()
        return carry

    lax.fori_loop(0, groups, finish, 0)


def shards(n, s, query_raw, query_tangent, key_raw, value_text, query_gain, key_gain):
    _, t, d = query_raw.shape
    _, c, fl = key_raw.shape
    groups = choose_groups(fl // HD)
    fg = fl // groups
    peers = max(s - 1, 1)
    lots = (groups + 1) // 2
    anywhere = pl.BlockSpec(memory_space=pl.ANY)
    flops = 2 * 4 * s * t * n * c * fl
    moved = 2 * (3 * t * d + 2 * c * fl)
    result = pl.pallas_call(
        functools.partial(kernel, n, s, groups),
        out_shape=jax.ShapeDtypeStruct((t, d), jnp.bfloat16),
        in_specs=[anywhere] * 6,
        out_specs=anywhere,
        scratch_shapes=[
            pltpu.VMEM((t, d), jnp.bfloat16),
            pltpu.VMEM((t, d), jnp.bfloat16),
            pltpu.VMEM((c, fl), jnp.bfloat16),
            pltpu.VMEM((1, d), jnp.float32),
            pltpu.VMEM((fl,), jnp.float32),
            pltpu.VMEM((groups, n, c, fg), jnp.bfloat16),
            pltpu.VMEM((groups, n, c, fg), jnp.bfloat16),
            pltpu.VMEM((peers, groups, 2, t, fg), jnp.bfloat16),
            pltpu.VMEM((groups, s, 2, t, fg), jnp.bfloat16),
            pltpu.VMEM((lots, s, 2, t, fg), jnp.bfloat16),
            pltpu.VMEM((groups, s, t, fg), jnp.bfloat16),
            pltpu.VMEM((lots, s, t, fg), jnp.bfloat16),
            pltpu.VMEM((s, c, HD), jnp.float32),
            pltpu.SemaphoreType.DMA((5,)),
            pltpu.SemaphoreType.DMA((groups,)),
            pltpu.SemaphoreType.DMA((2, 2, groups, n)),
            pltpu.SemaphoreType.DMA((2, groups, n)),
            pltpu.SemaphoreType.DMA((groups, peers)),
            pltpu.SemaphoreType.DMA((groups, peers)),
            pltpu.SemaphoreType.DMA((lots, s)),
            pltpu.SemaphoreType.DMA((lots, s)),
            pltpu.SemaphoreType.DMA((peers,)),
            pltpu.SemaphoreType.DMA((peers,)),
            pltpu.SemaphoreType.DMA((groups, peers)),
            pltpu.SemaphoreType.DMA((groups, s)),
            pltpu.SemaphoreType.DMA((lots, s)),
            pltpu.SemaphoreType.DMA((groups,)),
        ],
        compiler_params=pltpu.CompilerParams(
            collective_id=0, has_side_effects=True, vmem_limit_bytes=60 * 1024 * 1024
        ),
        cost_estimate=pl.CostEstimate(
            flops=flops, bytes_accessed=moved, transcendentals=s * t * n * c * (fl // HD)
        ),
    )(
        query_raw[0], query_tangent[0], key_raw[0], value_text[0],
        query_gain[None], key_gain,
    )
    return result[None]


def solution(mesh):
    n, s = mesh.shape["fsdp"], mesh.shape["sp"]
    return jax.shard_map(
        functools.partial(shards, n, s),
        mesh=mesh,
        in_specs=(
            P("dp", ("fsdp", "sp"), None),
            P("dp", ("fsdp", "sp"), None),
            P("dp", "fsdp", "sp"),
            P("dp", "fsdp", "sp"),
            P(),
            P("sp"),
        ),
        out_specs=P("dp", ("fsdp", "sp"), None),
        check_vma=False,
    )
```

```python
import functools

import jax
import jax.numpy as jnp
from jax import lax
from jax.experimental import pallas as pl
from jax.experimental.pallas import tpu as pltpu
from jax.sharding import PartitionSpec as P

HD = 128
LOG2E = 1.4426950408889634
epsilon = 1e-06
MESH = pl.DeviceIdType.MESH


def choose_groups(heads):
    for count in (10, 8, 6, 5, 4, 3, 2):
        if heads % count == 0:
            return count
    return 1


def kernel(
    n, s, groups,
    qr_hbm, qt_hbm, kr_hbm, v_ref, qg_hbm, kg_hbm, out_ref,
    qr_ref, qt_ref, kr_ref, qg_ref, kg_ref,
    kbuf, vbuf, qsend, qbuf, xbuf, obuf, ybuf, ssbuf,
    load_sem, vload_sem, kv_send, kv_recv, q_send, q_recv, x_send, x_recv,
    ss_send, ss_recv, o_send, o_recv, y_send, own_sem,
):
    t, d = qr_ref.shape
    inputs = ((kr_hbm, kr_ref), (kg_hbm, kg_ref), (qr_hbm, qr_ref), (qt_hbm, qt_ref), (qg_hbm, qg_ref))
    c, fl = kr_ref.shape
    fg = fl // groups
    per_group = fg // HD
    r = lax.axis_index("fsdp")
    p = lax.axis_index("sp")
    bufs = (kbuf, vbuf)

    def lot(g):
        return g // 2

    partner = jnp.where(r == 0, 1, jnp.where(r == 1, 0, jnp.where(r == n - 1, n - 2, n - 1)))

    def peer(dj):
        return lax.rem(p + dj, s)

    def origin(dj):
        return lax.rem(p + s - dj, s)

    def vload(g):
        columns = pl.ds(g * fg, fg)
        return pltpu.make_async_copy(v_ref.at[:, columns], vbuf.at[g, r], vload_sem.at[g])

    def piece(kind, g, src, way):
        target = r - 1 if way == 0 else r + 1
        buf = bufs[kind]
        return pltpu.make_async_remote_copy(
            src_ref=buf.at[g, src],
            dst_ref=buf.at[g, src],
            send_sem=kv_send.at[kind, way, g, src],
            recv_sem=kv_recv.at[kind, g, src],
            device_id={"fsdp": target},
            device_id_type=MESH,
        )

    def sums(dj):
        return pltpu.make_async_remote_copy(
            src_ref=ssbuf.at[0],
            dst_ref=ssbuf.at[dj],
            send_sem=ss_send.at[dj - 1],
            recv_sem=ss_recv.at[dj - 1],
            device_id={"sp": peer(dj)},
            device_id_type=MESH,
        )

    def queries(g, dj):
        return pltpu.make_async_remote_copy(
            src_ref=qsend.at[dj - 1, g],
            dst_ref=qbuf.at[g, dj],
            send_sem=q_send.at[g, dj - 1],
            recv_sem=q_recv.at[g, dj - 1],
            device_id={"sp": peer(dj)},
            device_id_type=MESH,
        )

    def lend(g, dj):
        return pltpu.make_async_remote_copy(
            src_ref=qbuf.at[g, dj],
            dst_ref=xbuf.at[lot(g), dj],
            send_sem=x_send.at[lot(g), dj],
            recv_sem=x_recv.at[lot(g), dj],
            device_id={"fsdp": partner},
            device_id_type=MESH,
        )

    def give_back(g, dj):
        columns = pl.ds(pl.multiple_of(p * fl + g * fg, HD), fg)
        return pltpu.make_async_remote_copy(
            src_ref=ybuf.at[lot(g), dj],
            dst_ref=out_ref.at[:, columns],
            send_sem=y_send.at[lot(g), dj],
            recv_sem=o_recv.at[g, dj],
            device_id={"fsdp": partner, "sp": origin(dj)},
            device_id_type=MESH,
        )

    def output(g, dj):
        columns = pl.ds(pl.multiple_of(p * fl + g * fg, HD), fg)
        return pltpu.make_async_remote_copy(
            src_ref=obuf.at[g, dj],
            dst_ref=out_ref.at[:, columns],
            send_sem=o_send.at[g, dj - 1],
            recv_sem=o_recv.at[g, dj],
            device_id={"sp": origin(dj)},
            device_id_type=MESH,
        )

    def own_output(g):
        columns = pl.ds(pl.multiple_of(p * fl + g * fg, HD), fg)
        return pltpu.make_async_copy(obuf.at[g, 0], out_ref.at[:, columns], own_sem.at[g])

    has_left = r > 0
    has_right = r < n - 1
    lending = n >= 4
    is_end = jnp.logical_or(r == 0, r == n - 1) if lending else r < 0
    is_helper = jnp.logical_or(r == 1, r == n - 2) if lending else r < 0

    def lent(g):
        return lax.rem(jnp.int32(g), 2) == 0

    def goes_left(g):
        return r > jnp.where(lent(g), 1, 0) if lending else has_left

    def goes_right(g):
        return r < jnp.where(lent(g), n - 2, n - 1) if lending else has_right

    def receives(g):
        return jnp.logical_not(jnp.logical_and(is_end, lent(g)))

    barrier = pltpu.get_barrier_semaphore()
    for dj in range(1, s):
        pl.semaphore_signal(barrier, inc=1, device_id={"sp": peer(dj)}, device_id_type=MESH)

    @pl.when(has_left)
    def _():
        pl.semaphore_signal(barrier, inc=1, device_id={"fsdp": r - 1}, device_id_type=MESH)

    @pl.when(has_right)
    def _():
        pl.semaphore_signal(barrier, inc=1, device_id={"fsdp": r + 1}, device_id_type=MESH)

    if s > 1:
        @pl.when(is_end)
        def _():
            for dj in range(1, s):
                pl.semaphore_signal(
                    barrier, inc=1, device_id={"fsdp": partner, "sp": peer(dj)}, device_id_type=MESH
                )

    loads = [pltpu.make_async_copy(a, b, load_sem.at[i]) for i, (a, b) in enumerate(inputs)]
    loads[0].start()
    for g in range(groups):
        vload(g).start()
    for load in loads[1:]:
        load.start()
    loads[0].wait()

    acc = jnp.zeros((c, HD), jnp.float32)
    for i in range(fl // HD):
        x = kr_ref[:, i * HD:(i + 1) * HD].astype(jnp.float32)
        acc = acc + x * x
    ssbuf[0] = jnp.broadcast_to(jnp.sum(acc, axis=-1, keepdims=True), (c, HD))

    pl.semaphore_wait(
        barrier,
        s - 1
        + has_left.astype(jnp.int32)
        + has_right.astype(jnp.int32)
        + (s - 1) * is_helper.astype(jnp.int32),
    )

    for dj in range(1, s):
        sums(dj).start()
    for g in range(groups):
        vload(g).wait()

    def send_own(kind, g):
        @pl.when(goes_left(g))
        def _():
            piece(kind, g, r, 0).start()

        @pl.when(goes_right(g))
        def _():
            piece(kind, g, r, 1).start()

    ahead = min(3, groups)
    for g in range(ahead):
        send_own(1, g)

    for dj in range(1, s):
        sums(dj).wait_recv()
    total = ssbuf[0]
    for dj in range(1, s):
        total = total + ssbuf[dj]
    loads[1].wait()
    key_inverse = lax.rsqrt(total * (1.0 / d) + epsilon)
    for g in range(groups):
        for i in range(per_group):
            lo = g * fg + i * HD
            x = kr_ref[:, lo:lo + HD].astype(jnp.float32)
            kbuf[g, r, :, i * HD:(i + 1) * HD] = (
                x * key_inverse * kg_ref[lo:lo + HD].reshape(1, HD)
            ).astype(jnp.bfloat16)
        if g < ahead:
            send_own(0, g)

    for load in loads[2:]:
        load.wait()
    square = jnp.zeros((t, HD), jnp.float32)
    cross = jnp.zeros((t, HD), jnp.float32)
    for i in range(d // HD):
        x = qr_ref[:, i * HD:(i + 1) * HD].astype(jnp.float32)
        y = qt_ref[:, i * HD:(i + 1) * HD].astype(jnp.float32)
        square = square + x * x
        cross = cross + x * y
    inverse = lax.rsqrt(jnp.sum(square, axis=-1, keepdims=True) * (1.0 / d) + epsilon)
    along = jnp.sum(cross, axis=-1, keepdims=True) * (1.0 / d)
    bend = inverse * inverse * along
    inverse = jnp.broadcast_to(inverse, (t, HD))
    bend = jnp.broadcast_to(bend, (t, HD))

    def norm_group(g, carry):
        for dj in [*range(1, s), 0]:
            j = peer(dj)
            for i in range(per_group):
                columns = pl.ds(pl.multiple_of(j * fl + g * fg + i * HD, HD), HD)
                x = qr_ref[:, columns].astype(jnp.float32)
                y = qt_ref[:, columns].astype(jnp.float32)
                gain = qg_ref[:, columns]
                primal = (x * inverse * gain).astype(jnp.bfloat16)
                tangent = (gain * inverse * (y - x * bend)).astype(jnp.bfloat16)
                if dj == 0:
                    qbuf[g, 0, 0, :, i * HD:(i + 1) * HD] = primal
                    qbuf[g, 0, 1, :, i * HD:(i + 1) * HD] = tangent
                else:
                    qsend[dj - 1, g, 0, :, i * HD:(i + 1) * HD] = primal
                    qsend[dj - 1, g, 1, :, i * HD:(i + 1) * HD] = tangent
            if dj > 0:
                queries(g, dj).start()
        return carry

    lax.fori_loop(0, groups, norm_group, 0)

    scale = HD ** (-0.5)

    def attend(g, i, rows_ref, place, into_ref, where):
        columns = slice(i * HD, (i + 1) * HD)
        keys = kbuf[g, :, :, columns].reshape(n * c, HD)
        values = vbuf[g, :, :, columns].reshape(n * c, HD)
        rows = rows_ref[place, :, :, :, columns].reshape(s * 2 * t, HD)
        paired = lax.dot_general(
            rows, keys, (((1,), (1,)), ((), ())), preferred_element_type=jnp.float32
        ).reshape(s, 2, t, n * c)
        tilts, factors = [], []
        for dj in range(s):
            scores, slopes = paired[dj, 0], paired[dj, 1]
            top = jnp.max(scores, axis=-1, keepdims=True)
            weights = jnp.exp2((scores - top) * (scale * LOG2E))
            whole = jnp.sum(weights, axis=-1, keepdims=True)
            mean = jnp.sum(weights * slopes, axis=-1, keepdims=True) / whole
            tilts.append((weights * (slopes - mean)).astype(jnp.bfloat16))
            factors.append(scale / whole)
        tilted = jnp.concatenate(tilts, axis=0)
        result = jnp.dot(tilted, values, preferred_element_type=jnp.float32)
        for dj in range(s):
            into_ref[where, dj, :, columns] = (
                result[dj * t:(dj + 1) * t] * factors[dj]
            ).astype(jnp.bfloat16)

    def launch(g):
        send_own(1, g)
        send_own(0, g)

    def lend_group(g):
        @pl.when(jnp.logical_and(is_end, lent(g)))
        def _():
            for dj in range(s):
                if dj > 0:
                    queries(g, dj).wait_recv()
                lend(g, dj).start()

    def forward(g, h):
        for kind in (1, 0):
            @pl.when(jnp.logical_and(r + h < n, receives(g)))
            def _():
                piece(kind, g, r + h, 0).wait_recv()

                @pl.when(goes_left(g))
                def _():
                    piece(kind, g, r + h, 0).start()

            @pl.when(jnp.logical_and(r - h >= 0, receives(g)))
            def _():
                piece(kind, g, r - h, 1).wait_recv()

                @pl.when(goes_right(g))
                def _():
                    piece(kind, g, r - h, 1).start()

    def work(g, i):
        @pl.when(receives(g))
        def _():
            if i == 0:
                for dj in range(1, s):
                    queries(g, dj).wait_recv()
            attend(g, i, qbuf, g, obuf, g)
            if i == per_group - 1:
                for dj in range(1, s):
                    output(g, dj).start()
                own_output(g).start()

    def help_end(g, i):
        @pl.when(jnp.logical_and(is_helper, lent(g)))
        def _():
            if i == 0:
                for dj in range(s):
                    lend(g, dj).wait_recv()
            attend(g, i, xbuf, lot(g), ybuf, lot(g))
            if i == per_group - 1:
                for dj in range(s):
                    give_back(g, dj).start()

    for g in range(ahead):
        lend_group(g)

    lead, lag = 1, 2

    def step(i, carry):
        @pl.when(i + ahead < groups)
        def _():
            launch(i + ahead)
            lend_group(i + ahead)

        moves = list(range(1, n))
        units = [(work, lead, k) for k in range(per_group)]
        units += [(help_end, lag, k) for k in range(per_group)]
        for k in range(max(len(moves), len(units))):
            if k < len(moves):
                @pl.when(i < groups)
                def _():
                    forward(i, moves[k])

            if k < len(units):
                unit, behind, part = units[k]

                @pl.when(jnp.logical_and(i >= behind, i - behind < groups))
                def _():
                    unit(i - behind, part)

        return carry

    lax.fori_loop(0, max(groups + lead, groups - 1 + lag), step, 0)

    for dj in range(1, s):
        sums(dj).wait_send()

    def finish(g, carry):
        for kind in (1, 0):
            for h in range(n):
                @pl.when(jnp.logical_and(r + h < n, goes_left(g)) if h == 0 else
                         jnp.logical_and(jnp.logical_and(r + h < n, goes_left(g)), receives(g)))
                def _():
                    piece(kind, g, r + h, 0).wait_send()

                @pl.when(jnp.logical_and(r - h >= 0, goes_right(g)) if h == 0 else
                         jnp.logical_and(jnp.logical_and(r - h >= 0, goes_right(g)), receives(g)))
                def _():
                    piece(kind, g, r - h, 1).wait_send()

        for dj in range(1, s):
            queries(g, dj).wait_send()
            output(g, dj).wait_recv()

        @pl.when(receives(g))
        def _():
            own_output(g).wait()
            for dj in range(1, s):
                output(g, dj).wait_send()

        @pl.when(jnp.logical_and(is_end, lent(g)))
        def _():
            for dj in range(s):
                lend(g, dj).wait_send()
            give_back(g, 0).wait_recv()

        @pl.when(jnp.logical_and(is_helper, lent(g)))
        def _():
            for dj in range(s):
                give_back(g, dj).wait_send()
        return carry

    lax.fori_loop(0, groups, finish, 0)


def shards(n, s, query_raw, query_tangent, key_raw, value_text, query_gain, key_gain):
    _, t, d = query_raw.shape
    _, c, fl = key_raw.shape
    groups = choose_groups(fl // HD)
    fg = fl // groups
    peers = max(s - 1, 1)
    lots = groups // 2 + 1
    anywhere = pl.BlockSpec(memory_space=pl.ANY)
    flops = 2 * 4 * s * t * n * c * fl
    moved = 2 * (3 * t * d + 2 * c * fl)
    result = pl.pallas_call(
        functools.partial(kernel, n, s, groups),
        out_shape=jax.ShapeDtypeStruct((t, d), jnp.bfloat16),
        in_specs=[anywhere] * 6,
        out_specs=anywhere,
        scratch_shapes=[
            pltpu.VMEM((t, d), jnp.bfloat16),
            pltpu.VMEM((t, d), jnp.bfloat16),
            pltpu.VMEM((c, fl), jnp.bfloat16),
            pltpu.VMEM((1, d), jnp.float32),
            pltpu.VMEM((fl,), jnp.float32),
            pltpu.VMEM((groups, n, c, fg), jnp.bfloat16),
            pltpu.VMEM((groups, n, c, fg), jnp.bfloat16),
            pltpu.VMEM((peers, groups, 2, t, fg), jnp.bfloat16),
            pltpu.VMEM((groups, s, 2, t, fg), jnp.bfloat16),
            pltpu.VMEM((lots, s, 2, t, fg), jnp.bfloat16),
            pltpu.VMEM((groups, s, t, fg), jnp.bfloat16),
            pltpu.VMEM((lots, s, t, fg), jnp.bfloat16),
            pltpu.VMEM((s, c, HD), jnp.float32),
            pltpu.SemaphoreType.DMA((5,)),
            pltpu.SemaphoreType.DMA((groups,)),
            pltpu.SemaphoreType.DMA((2, 2, groups, n)),
            pltpu.SemaphoreType.DMA((2, groups, n)),
            pltpu.SemaphoreType.DMA((groups, peers)),
            pltpu.SemaphoreType.DMA((groups, peers)),
            pltpu.SemaphoreType.DMA((lots, s)),
            pltpu.SemaphoreType.DMA((lots, s)),
            pltpu.SemaphoreType.DMA((peers,)),
            pltpu.SemaphoreType.DMA((peers,)),
            pltpu.SemaphoreType.DMA((groups, peers)),
            pltpu.SemaphoreType.DMA((groups, s)),
            pltpu.SemaphoreType.DMA((lots, s)),
            pltpu.SemaphoreType.DMA((groups,)),
        ],
        compiler_params=pltpu.CompilerParams(
            collective_id=0, has_side_effects=True, vmem_limit_bytes=60 * 1024 * 1024
        ),
        cost_estimate=pl.CostEstimate(
            flops=flops, bytes_accessed=moved, transcendentals=s * t * n * c * (fl // HD)
        ),
    )(
        query_raw[0], query_tangent[0], key_raw[0], value_text[0],
        query_gain[None], key_gain,
    )
    return result[None]


def solution(mesh):
    n, s = mesh.shape["fsdp"], mesh.shape["sp"]
    return jax.shard_map(
        functools.partial(shards, n, s),
        mesh=mesh,
        in_specs=(
            P("dp", ("fsdp", "sp"), None),
            P("dp", ("fsdp", "sp"), None),
            P("dp", "fsdp", "sp"),
            P("dp", "fsdp", "sp"),
            P(),
            P("sp"),
        ),
        out_specs=P("dp", ("fsdp", "sp"), None),
        check_vma=False,
    )
```

```python
import functools

import jax
import jax.numpy as jnp
from jax import lax
from jax.experimental import pallas as pl
from jax.experimental.pallas import tpu as pltpu
from jax.sharding import PartitionSpec as P

HD = 128
LOG2E = 1.4426950408889634
epsilon = 1e-06
MESH = pl.DeviceIdType.MESH


def choose_groups(heads):
    for count in (10, 8, 6, 5, 4, 3, 2):
        if heads % count == 0:
            return count
    return 1


def kernel(
    n, s, groups,
    qr_hbm, qt_hbm, kr_hbm, v_ref, qg_hbm, kg_hbm, out_ref,
    qr_ref, qt_ref, kr_ref, qg_ref, kg_ref,
    kbuf, vbuf, qsend, qbuf, xbuf, obuf, ybuf, ssbuf,
    load_sem, vload_sem, kv_send, kv_recv, q_send, q_recv, x_send, x_recv,
    ss_send, ss_recv, o_send, o_recv, y_send, own_sem,
):
    t, d = qr_ref.shape
    inputs = ((kr_hbm, kr_ref), (kg_hbm, kg_ref), (qr_hbm, qr_ref), (qt_hbm, qt_ref), (qg_hbm, qg_ref))
    c, fl = kr_ref.shape
    fg = fl // groups
    per_group = fg // HD
    r = lax.axis_index("fsdp")
    p = lax.axis_index("sp")
    bufs = (kbuf, vbuf)

    def lot(g):
        return g

    partner = jnp.where(r == 0, 1, jnp.where(r == 1, 0, jnp.where(r == n - 1, n - 2, n - 1)))

    def peer(dj):
        return lax.rem(p + dj, s)

    def origin(dj):
        return lax.rem(p + s - dj, s)

    def vload(g):
        columns = pl.ds(g * fg, fg)
        return pltpu.make_async_copy(v_ref.at[:, columns], vbuf.at[g, r], vload_sem.at[g])

    def piece(kind, g, src, way):
        target = r - 1 if way == 0 else r + 1
        buf = bufs[kind]
        return pltpu.make_async_remote_copy(
            src_ref=buf.at[g, src],
            dst_ref=buf.at[g, src],
            send_sem=kv_send.at[kind, way, g, src],
            recv_sem=kv_recv.at[kind, g, src],
            device_id={"fsdp": target},
            device_id_type=MESH,
        )

    def sums(dj):
        return pltpu.make_async_remote_copy(
            src_ref=ssbuf.at[0],
            dst_ref=ssbuf.at[dj],
            send_sem=ss_send.at[dj - 1],
            recv_sem=ss_recv.at[dj - 1],
            device_id={"sp": peer(dj)},
            device_id_type=MESH,
        )

    def queries(g, dj):
        return pltpu.make_async_remote_copy(
            src_ref=qsend.at[dj - 1, g],
            dst_ref=qbuf.at[g, dj],
            send_sem=q_send.at[g, dj - 1],
            recv_sem=q_recv.at[g, dj - 1],
            device_id={"sp": peer(dj)},
            device_id_type=MESH,
        )

    def lend(g, dj):
        return pltpu.make_async_remote_copy(
            src_ref=qbuf.at[g, dj],
            dst_ref=xbuf.at[lot(g), dj],
            send_sem=x_send.at[lot(g), dj],
            recv_sem=x_recv.at[lot(g), dj],
            device_id={"fsdp": partner},
            device_id_type=MESH,
        )

    def give_back(g, dj):
        columns = pl.ds(pl.multiple_of(p * fl + g * fg, HD), fg)
        return pltpu.make_async_remote_copy(
            src_ref=ybuf.at[lot(g), dj],
            dst_ref=out_ref.at[:, columns],
            send_sem=y_send.at[lot(g), dj],
            recv_sem=o_recv.at[g, dj],
            device_id={"fsdp": partner, "sp": origin(dj)},
            device_id_type=MESH,
        )

    def output(g, dj):
        columns = pl.ds(pl.multiple_of(p * fl + g * fg, HD), fg)
        return pltpu.make_async_remote_copy(
            src_ref=obuf.at[g, dj],
            dst_ref=out_ref.at[:, columns],
            send_sem=o_send.at[g, dj - 1],
            recv_sem=o_recv.at[g, dj],
            device_id={"sp": origin(dj)},
            device_id_type=MESH,
        )

    def own_output(g):
        columns = pl.ds(pl.multiple_of(p * fl + g * fg, HD), fg)
        return pltpu.make_async_copy(obuf.at[g, 0], out_ref.at[:, columns], own_sem.at[g])

    has_left = r > 0
    has_right = r < n - 1
    lending = n >= 4
    is_end = jnp.logical_or(r == 0, r == n - 1) if lending else r < 0
    is_helper = jnp.logical_or(r == 1, r == n - 2) if lending else r < 0

    def lent(g):
        return lax.rem(jnp.int32(g), 2) == 1

    def goes_left(g):
        return r > jnp.where(lent(g), 1, 0) if lending else has_left

    def goes_right(g):
        return r < jnp.where(lent(g), n - 2, n - 1) if lending else has_right

    def receives(g):
        return jnp.logical_not(jnp.logical_and(is_end, lent(g)))

    barrier = pltpu.get_barrier_semaphore()
    for dj in range(1, s):
        pl.semaphore_signal(barrier, inc=1, device_id={"sp": peer(dj)}, device_id_type=MESH)

    @pl.when(has_left)
    def _():
        pl.semaphore_signal(barrier, inc=1, device_id={"fsdp": r - 1}, device_id_type=MESH)

    @pl.when(has_right)
    def _():
        pl.semaphore_signal(barrier, inc=1, device_id={"fsdp": r + 1}, device_id_type=MESH)

    if s > 1:
        @pl.when(is_end)
        def _():
            for dj in range(1, s):
                pl.semaphore_signal(
                    barrier, inc=1, device_id={"fsdp": partner, "sp": peer(dj)}, device_id_type=MESH
                )

    loads = [pltpu.make_async_copy(a, b, load_sem.at[i]) for i, (a, b) in enumerate(inputs)]
    loads[0].start()
    for g in range(groups):
        vload(g).start()
    for load in loads[1:]:
        load.start()
    loads[0].wait()

    acc = jnp.zeros((c, HD), jnp.float32)
    for i in range(fl // HD):
        x = kr_ref[:, i * HD:(i + 1) * HD].astype(jnp.float32)
        acc = acc + x * x
    ssbuf[0] = jnp.broadcast_to(jnp.sum(acc, axis=-1, keepdims=True), (c, HD))

    pl.semaphore_wait(
        barrier,
        s - 1
        + has_left.astype(jnp.int32)
        + has_right.astype(jnp.int32)
        + (s - 1) * is_helper.astype(jnp.int32),
    )

    for dj in range(1, s):
        sums(dj).start()
    for g in range(groups):
        vload(g).wait()

    def send_own(kind, g):
        @pl.when(goes_left(g))
        def _():
            piece(kind, g, r, 0).start()

        @pl.when(goes_right(g))
        def _():
            piece(kind, g, r, 1).start()

    ahead = min(3, groups)
    for g in range(ahead):
        send_own(1, g)

    for dj in range(1, s):
        sums(dj).wait_recv()
    total = ssbuf[0]
    for dj in range(1, s):
        total = total + ssbuf[dj]
    loads[1].wait()
    key_inverse = lax.rsqrt(total * (1.0 / d) + epsilon)
    for g in range(groups):
        for i in range(per_group):
            lo = g * fg + i * HD
            x = kr_ref[:, lo:lo + HD].astype(jnp.float32)
            kbuf[g, r, :, i * HD:(i + 1) * HD] = (
                x * key_inverse * kg_ref[lo:lo + HD].reshape(1, HD)
            ).astype(jnp.bfloat16)
        if g < ahead:
            send_own(0, g)

    for load in loads[2:]:
        load.wait()
    square = jnp.zeros((t, HD), jnp.float32)
    cross = jnp.zeros((t, HD), jnp.float32)
    for i in range(d // HD):
        x = qr_ref[:, i * HD:(i + 1) * HD].astype(jnp.float32)
        y = qt_ref[:, i * HD:(i + 1) * HD].astype(jnp.float32)
        square = square + x * x
        cross = cross + x * y
    inverse = lax.rsqrt(jnp.sum(square, axis=-1, keepdims=True) * (1.0 / d) + epsilon)
    along = jnp.sum(cross, axis=-1, keepdims=True) * (1.0 / d)
    bend = inverse * inverse * along
    inverse = jnp.broadcast_to(inverse, (t, HD))
    bend = jnp.broadcast_to(bend, (t, HD))

    def norm_group(g, carry):
        for dj in [*range(1, s), 0]:
            j = peer(dj)
            for i in range(per_group):
                columns = pl.ds(pl.multiple_of(j * fl + g * fg + i * HD, HD), HD)
                x = qr_ref[:, columns].astype(jnp.float32)
                y = qt_ref[:, columns].astype(jnp.float32)
                gain = qg_ref[:, columns]
                primal = (x * inverse * gain).astype(jnp.bfloat16)
                tangent = (gain * inverse * (y - x * bend)).astype(jnp.bfloat16)
                if dj == 0:
                    qbuf[g, 0, 0, :, i * HD:(i + 1) * HD] = primal
                    qbuf[g, 0, 1, :, i * HD:(i + 1) * HD] = tangent
                else:
                    qsend[dj - 1, g, 0, :, i * HD:(i + 1) * HD] = primal
                    qsend[dj - 1, g, 1, :, i * HD:(i + 1) * HD] = tangent
            if dj > 0:
                queries(g, dj).start()
        return carry

    lax.fori_loop(0, groups, norm_group, 0)

    scale = HD ** (-0.5)

    def attend(g, i, rows_ref, place, into_ref, where):
        columns = slice(i * HD, (i + 1) * HD)
        keys = kbuf[g, :, :, columns].reshape(n * c, HD)
        values = vbuf[g, :, :, columns].reshape(n * c, HD)
        rows = rows_ref[place, :, :, :, columns].reshape(s * 2 * t, HD)
        paired = lax.dot_general(
            rows, keys, (((1,), (1,)), ((), ())), preferred_element_type=jnp.float32
        ).reshape(s, 2, t, n * c)
        tilts, factors = [], []
        for dj in range(s):
            scores, slopes = paired[dj, 0], paired[dj, 1]
            top = jnp.max(scores, axis=-1, keepdims=True)
            weights = jnp.exp2((scores - top) * (scale * LOG2E))
            whole = jnp.sum(weights, axis=-1, keepdims=True)
            mean = jnp.sum(weights * slopes, axis=-1, keepdims=True) / whole
            tilts.append((weights * (slopes - mean)).astype(jnp.bfloat16))
            factors.append(scale / whole)
        tilted = jnp.concatenate(tilts, axis=0)
        result = jnp.dot(tilted, values, preferred_element_type=jnp.float32)
        for dj in range(s):
            into_ref[where, dj, :, columns] = (
                result[dj * t:(dj + 1) * t] * factors[dj]
            ).astype(jnp.bfloat16)

    def launch(g):
        send_own(1, g)
        send_own(0, g)

    def lend_group(g):
        @pl.when(jnp.logical_and(is_end, lent(g)))
        def _():
            for dj in range(s):
                if dj > 0:
                    queries(g, dj).wait_recv()
                lend(g, dj).start()

    def forward(g, h):
        for kind in (1, 0):
            @pl.when(jnp.logical_and(r + h < n, receives(g)))
            def _():
                piece(kind, g, r + h, 0).wait_recv()

                @pl.when(goes_left(g))
                def _():
                    piece(kind, g, r + h, 0).start()

            @pl.when(jnp.logical_and(r - h >= 0, receives(g)))
            def _():
                piece(kind, g, r - h, 1).wait_recv()

                @pl.when(goes_right(g))
                def _():
                    piece(kind, g, r - h, 1).start()

    def work(g, i):
        @pl.when(receives(g))
        def _():
            if i == 0:
                for dj in range(1, s):
                    queries(g, dj).wait_recv()
            attend(g, i, qbuf, g, obuf, g)
            if i == per_group - 1:
                for dj in range(1, s):
                    output(g, dj).start()
                own_output(g).start()

    def help_end(g, i):
        @pl.when(jnp.logical_and(is_helper, lent(g)))
        def _():
            if i == 0:
                for dj in range(s):
                    lend(g, dj).wait_recv()
            attend(g, i, xbuf, lot(g), ybuf, lot(g))
            if i == per_group - 1:
                for dj in range(s):
                    give_back(g, dj).start()

    for g in range(ahead):
        lend_group(g)

    lead, lag = 1, 1

    def step(i, carry):
        @pl.when(i + ahead < groups)
        def _():
            launch(i + ahead)
            lend_group(i + ahead)

        moves = list(range(1, n))
        units = [(work, lead, k) for k in range(per_group)]
        units += [(help_end, lag, k) for k in range(per_group)]
        for k in range(max(len(moves), len(units))):
            if k < len(moves):
                @pl.when(i < groups)
                def _():
                    forward(i, moves[k])

            if k < len(units):
                unit, behind, part = units[k]

                @pl.when(jnp.logical_and(i >= behind, i - behind < groups))
                def _():
                    unit(i - behind, part)

        return carry

    lax.fori_loop(0, max(groups + lead, groups - 1 + lag), step, 0)

    for dj in range(1, s):
        sums(dj).wait_send()

    def finish(g, carry):
        for kind in (1, 0):
            for h in range(n):
                @pl.when(jnp.logical_and(r + h < n, goes_left(g)) if h == 0 else
                         jnp.logical_and(jnp.logical_and(r + h < n, goes_left(g)), receives(g)))
                def _():
                    piece(kind, g, r + h, 0).wait_send()

                @pl.when(jnp.logical_and(r - h >= 0, goes_right(g)) if h == 0 else
                         jnp.logical_and(jnp.logical_and(r - h >= 0, goes_right(g)), receives(g)))
                def _():
                    piece(kind, g, r - h, 1).wait_send()

        for dj in range(1, s):
            queries(g, dj).wait_send()
            output(g, dj).wait_recv()

        @pl.when(receives(g))
        def _():
            own_output(g).wait()
            for dj in range(1, s):
                output(g, dj).wait_send()

        @pl.when(jnp.logical_and(is_end, lent(g)))
        def _():
            for dj in range(s):
                lend(g, dj).wait_send()
            give_back(g, 0).wait_recv()

        @pl.when(jnp.logical_and(is_helper, lent(g)))
        def _():
            for dj in range(s):
                give_back(g, dj).wait_send()
        return carry

    lax.fori_loop(0, groups, finish, 0)


def shards(n, s, query_raw, query_tangent, key_raw, value_text, query_gain, key_gain):
    _, t, d = query_raw.shape
    _, c, fl = key_raw.shape
    groups = choose_groups(fl // HD)
    fg = fl // groups
    peers = max(s - 1, 1)
    lots = groups
    anywhere = pl.BlockSpec(memory_space=pl.ANY)
    flops = 2 * 4 * s * t * n * c * fl
    moved = 2 * (3 * t * d + 2 * c * fl)
    result = pl.pallas_call(
        functools.partial(kernel, n, s, groups),
        out_shape=jax.ShapeDtypeStruct((t, d), jnp.bfloat16),
        in_specs=[anywhere] * 6,
        out_specs=anywhere,
        scratch_shapes=[
            pltpu.VMEM((t, d), jnp.bfloat16),
            pltpu.VMEM((t, d), jnp.bfloat16),
            pltpu.VMEM((c, fl), jnp.bfloat16),
            pltpu.VMEM((1, d), jnp.float32),
            pltpu.VMEM((fl,), jnp.float32),
            pltpu.VMEM((groups, n, c, fg), jnp.bfloat16),
            pltpu.VMEM((groups, n, c, fg), jnp.bfloat16),
            pltpu.VMEM((peers, groups, 2, t, fg), jnp.bfloat16),
            pltpu.VMEM((groups, s, 2, t, fg), jnp.bfloat16),
            pltpu.VMEM((lots, s, 2, t, fg), jnp.bfloat16),
            pltpu.VMEM((groups, s, t, fg), jnp.bfloat16),
            pltpu.VMEM((lots, s, t, fg), jnp.bfloat16),
            pltpu.VMEM((s, c, HD), jnp.float32),
            pltpu.SemaphoreType.DMA((5,)),
            pltpu.SemaphoreType.DMA((groups,)),
            pltpu.SemaphoreType.DMA((2, 2, groups, n)),
            pltpu.SemaphoreType.DMA((2, groups, n)),
            pltpu.SemaphoreType.DMA((groups, peers)),
            pltpu.SemaphoreType.DMA((groups, peers)),
            pltpu.SemaphoreType.DMA((lots, s)),
            pltpu.SemaphoreType.DMA((lots, s)),
            pltpu.SemaphoreType.DMA((peers,)),
            pltpu.SemaphoreType.DMA((peers,)),
            pltpu.SemaphoreType.DMA((groups, peers)),
            pltpu.SemaphoreType.DMA((groups, s)),
            pltpu.SemaphoreType.DMA((lots, s)),
            pltpu.SemaphoreType.DMA((groups,)),
        ],
        compiler_params=pltpu.CompilerParams(
            collective_id=0, has_side_effects=True, vmem_limit_bytes=60 * 1024 * 1024
        ),
        cost_estimate=pl.CostEstimate(
            flops=flops, bytes_accessed=moved, transcendentals=s * t * n * c * (fl // HD)
        ),
    )(
        query_raw[0], query_tangent[0], key_raw[0], value_text[0],
        query_gain[None], key_gain,
    )
    return result[None]


def solution(mesh):
    n, s = mesh.shape["fsdp"], mesh.shape["sp"]
    return jax.shard_map(
        functools.partial(shards, n, s),
        mesh=mesh,
        in_specs=(
            P("dp", ("fsdp", "sp"), None),
            P("dp", ("fsdp", "sp"), None),
            P("dp", "fsdp", "sp"),
            P("dp", "fsdp", "sp"),
            P(),
            P("sp"),
        ),
        out_specs=P("dp", ("fsdp", "sp"), None),
        check_vma=False,
    )
```
